32 devices in a mesh: section: 4 (over x, core), expert: 2 (over y), dp: 4 (over z).
Axes of the slice: x: 2, y: 2, z: 4, core: 2. Of those that a mesh axis runs over, the one named last changes fastest.
Arguments:
- in_flight: bfloat16 [4, 2, 128, 3584], P('section', None, 'expert', 'dp'), may hold values from -6 to 6
- incoming: bfloat16 [2, 128, 3584], P(None, 'expert', 'dp'), may hold values from -6 to 6
- up_proj: bfloat16 [4, 32, 3584, 1152], P('section', 'expert', 'dp'), may hold values from -0.09375 to 0.09375
- down_proj: bfloat16 [4, 32, 1152, 3584], P('section', 'expert', None, 'dp'), may hold values from -0.1875 to 0.1875
- expert_ids: int32 [2, 4, 2, 128, 4], P(None, 'section', None, 'expert'), may hold values from 0 to 31, all different within a row; in each aligned block of 64 rows (0 to 63, 64 to 127, ..., all dimensions but the last counted through in order) at most 12 rows name the same one
- gate_logits: float32 [2, 4, 2, 128, 4], P(None, 'section', None, 'expert'), may hold values from -6 to 6
Outputs:
- states: bfloat16 [2, 4, 2, 128, 3584], P(None, 'section', None, 'expert', 'dp')
The draws below stay inside these ranges and needn't reach their ends.
Inputs may be any that keep to these rules, and one draw needn't show every extreme that they name: `expert_ids`: each row names 4 different experts. In every aligned block of 64 rows, no expert is named by more than 12 rows, a bound that some block reaches.
All inputs are finite; a program needn't handle non-finite values.
Results may differ from the reference program's by a relative error of at most 0.015.
Values may be sent and summed in bfloat16 or wider, within the bound.
A program may use at most 192 MiB of HBM per device.

```python
import math
import jax
import jax.numpy as jnp
import numpy as np
from jax import lax

D = 3584
FF = 1152
MROWS = 64
MB = 2
TICKS = 2
TOP = 4
EXPERTS = 32
CAP = 12
TOK_MB = 128
N_SECTION = 4
N_EXPERT = 2
N_DP = 4


def steps_of(own_key, dims, shards, low, top_value):
    factor_of = 1.0
    for dim, parts in shards:
        steps = jax.random.uniform(jax.random.fold_in(jax.random.fold_in(own_key, 6), dim), (parts,), jnp.float32, low / len(shards), top_value / len(shards))
        factor_of = factor_of * jnp.repeat(jnp.exp(steps), dims[dim] // parts).reshape((-1,) + (1,) * (len(dims) - 1 - dim))
    return factor_of


def deal_out(key, own, number, rows, amount, top, reach, lean):
    order = jax.random.permutation(key, amount)
    packed, ordinary = load_shares(amount, rows * top, reach, lean, True), load_shares(amount, rows * top, reach, lean, False)
    places = jnp.arange(amount)

    def named(lengths, offset_by):
        used = int((lengths > 0).sum())
        fixed = max(1, used // 4)
        moved = fixed + (places - fixed + offset_by * (used - fixed)) % max(1, amount - fixed)
        return jnp.zeros((amount,), jnp.int32).at[order[jnp.where(places < fixed, places, moved)]].set(jnp.asarray(lengths, jnp.int32))

    lengths = jnp.where(number % 4 == 0, named(packed, number // 4), named(ordinary, number - number // 4 - 1))
    mixed = jax.random.permutation(jax.random.fold_in(own, 3), amount)
    donor, taker = mixed[0:amount // 2 * 2:2], mixed[1:amount // 2 * 2:2]
    slack = jnp.minimum(lengths[donor] - 1, reach - lengths[taker]) // 2
    slack = jnp.where((donor == order[0]) | (taker == order[0]) | (lengths[taker] == 0), 0, jnp.maximum(slack, 0))
    moved = jax.random.randint(jax.random.fold_in(own, 4), (amount // 2,), 0, 1 << 20) % (slack + 1)
    lengths = lengths.at[donor].add(-moved).at[taker].add(moved)
    members = jnp.searchsorted(jnp.cumsum(lengths), jnp.arange(rows * top), side="right").astype(jnp.int32)
    table = members.reshape(top, rows).T
    table = table[jax.random.permutation(jax.random.fold_in(own, 1), rows)]
    offset_by = jax.random.randint(jax.random.fold_in(own, 2), (rows, 1), 0, top)
    return jnp.take_along_axis(table, (jnp.arange(top)[None, :] + offset_by) % top, axis=1)


def load_shares(count, total, reach, lean, full):
    loads = [(1 << 20) // math.isqrt(rank ** lean) + 1 for rank in range(1, count + 1)]
    largest = reach if full else min(reach, max(-(-total // count), total * loads[0] // sum(loads)))
    least = 1 if total - largest >= count - 1 else 0
    counts, spare = [largest] + [least] * (count - 1), total - largest - least * (count - 1)
    while spare > 0:
        candidates = [i for i in range(1, count) if counts[i] < largest] or [i for i in range(1, count) if counts[i] < reach]
        mass, remaining = sum([loads[i] for i in candidates]), spare
        for i in candidates:
            extra = min(reach - counts[i], max(1, remaining * loads[i] // mass), spare)
            counts[i] = counts[i] + extra
            spare = spare - extra
    return np.array(counts)


def scatter_about(rng, shape, spread, bound, pieces=(), held_as=jnp.bfloat16):
    result = spread * jax.random.normal(rng, shape, jnp.float32)
    if pieces:
        result = result * steps_of(rng, shape, pieces, -0.22, 0.18)
    return jnp.clip(result, -bound, bound).astype(held_as)


def setup_inputs(seed: int = 0) -> dict:
    splits = jax.random.split(jax.random.key(seed), 7)
    in_flight = scatter_about(splits[0], (N_SECTION, MB, TOK_MB, D), 1.0, 6.0, ((0, 4), (2, 2), (3, 4)))
    incoming = scatter_about(splits[1], (MB, TOK_MB, D), 1.0, 6.0, ((1, 2), (2, 4)))
    up_proj = scatter_about(splits[2], (N_SECTION, EXPERTS, D, FF), D ** -0.5, 0.09375, ((0, 4), (1, 2), (2, 4)))
    down_proj = scatter_about(splits[3], (N_SECTION, EXPERTS, FF, D), FF ** -0.5, 0.1875, ((0, 4), (1, 2), (3, 4)))
    expert_ids_keys = jax.random.split(jax.random.fold_in(splits[4], 1), TICKS * N_SECTION * MB * TOK_MB // MROWS)
    expert_ids_turns = jax.random.permutation(jax.random.fold_in(splits[4], 3), TICKS * N_SECTION * MB * TOK_MB // MROWS)
    expert_ids = jax.vmap(lambda own, number: deal_out(jax.random.fold_in(splits[4], 2), own, number, MROWS, EXPERTS, TOP, CAP, 2))(expert_ids_keys, expert_ids_turns).reshape((TICKS, N_SECTION, MB, TOK_MB, TOP))
    gate_logits = scatter_about(splits[5], (TICKS, N_SECTION, MB, TOK_MB, TOP), 1.5, 6.0, ((1, 4), (3, 2)), jnp.float32)
    return {"in_flight": in_flight, "incoming": incoming, "up_proj": up_proj, "down_proj": down_proj, "expert_ids": expert_ids, "gate_logits": gate_logits}


def gate_weights(logits):
    squashed = jax.nn.sigmoid(logits)
    return 2.5 * squashed / jnp.sum(squashed, axis=-1, keepdims=True)


def slot_table(routing):
    blocks = routing.reshape(N_EXPERT, MROWS * TOP)
    onehot = (blocks[:, :, None] == jnp.arange(EXPERTS, dtype=jnp.int32)[None, None, :]).astype(jnp.int32)
    before = jnp.cumsum(onehot, axis=1) - onehot
    return jnp.sum(before * onehot, axis=2)


def run_expert(operands):
    rows_in, up_weight, down_weight = operands
    quarter = D // N_DP
    partial_value = jnp.zeros((rows_in.shape[0], FF), jnp.float32)
    for quarter_index in range(N_DP):
        lower = quarter_index * quarter
        product = jnp.dot(rows_in[:, lower:lower + quarter], up_weight[lower:lower + quarter], preferred_element_type=jnp.float32)
        rounded = lax.optimization_barrier(product.astype(jnp.bfloat16))
        partial_value = partial_value + rounded.astype(jnp.float32)
    hidden = jax.nn.silu(partial_value).astype(jnp.bfloat16)
    return jnp.dot(hidden, down_weight, preferred_element_type=jnp.float32).astype(jnp.bfloat16)


def moe_layer(tokens_in, routing, logits, up_weight, down_weight):
    slot_numbers = slot_table(routing)
    owner_block = jnp.arange(N_EXPERT, dtype=jnp.int32)[:, None]
    pair_ids = routing.reshape(N_EXPERT, MROWS * TOP)
    slot_index = (pair_ids * (N_EXPERT * CAP) + owner_block * CAP + slot_numbers).reshape(-1)
    row_ids = jnp.broadcast_to(jnp.arange(TOK_MB, dtype=jnp.int32)[:, None], (TOK_MB, TOP)).reshape(-1)
    source = jnp.full((EXPERTS * N_EXPERT * CAP,), -1, jnp.int32).at[slot_index].set(row_ids)
    filled = source >= 0
    buffer = jnp.where(filled[:, None], tokens_in[jnp.maximum(source, 0)], jnp.zeros((), tokens_in.dtype))
    buffer = buffer.reshape(EXPERTS, N_EXPERT * CAP, D)
    outputs = lax.map(run_expert, (buffer, up_weight, down_weight)).reshape(EXPERTS * N_EXPERT * CAP, D)
    picked = outputs[slot_index].reshape(TOK_MB, TOP, D).astype(jnp.float32)
    weights = gate_weights(logits)
    routed_sum = jnp.sum(weights[:, :, None] * picked, axis=1)
    return (tokens_in.astype(jnp.float32) + routed_sum).astype(jnp.bfloat16)


def reference(in_flight, incoming, up_proj, down_proj, expert_ids, gate_logits):
    current = in_flight
    results = []
    for tick_index in range(TICKS):
        if tick_index > 0:
            previous = results[-1]
            current = jnp.concatenate([incoming[None], previous[:-1]], axis=0)
        section_outputs = []
        for section_index in range(N_SECTION):
            per_batch = []
            for micro_index in range(MB):
                per_batch.append(moe_layer(current[section_index, micro_index], expert_ids[tick_index, section_index, micro_index], gate_logits[tick_index, section_index, micro_index], up_proj[section_index], down_proj[section_index]))
            section_outputs.append(jnp.stack(per_batch))
        results.append(jnp.stack(section_outputs))
    return jnp.stack(results)
```

```python
import functools

import jax
import jax.numpy as jnp
from jax import lax
from jax.experimental import pallas as pl
from jax.experimental.pallas import tpu as pltpu
from jax.sharding import PartitionSpec as P

MB = 2
TICKS = 2
TOP = 4


def shifted(block, axis, distance):
    devices = range(lax.axis_size(axis))
    route = [(i - distance, i) for i in devices if i - distance in devices]
    return lax.ppermute(block, axis, route)


def gate_weights(logits):
    squashed = jax.nn.sigmoid(logits)
    return 2.5 * squashed / jnp.sum(squashed, axis=-1, keepdims=True)


def routing_slots(routing, experts, capacity):
    pair_ids = routing.reshape(-1)
    onehot = (pair_ids[:, None] == jnp.arange(experts, dtype=jnp.int32)[None, :]).astype(jnp.int32)
    earlier = jnp.tri(pair_ids.shape[0], k=-1, dtype=jnp.bfloat16)
    before = jnp.dot(
        earlier, onehot.astype(jnp.bfloat16), preferred_element_type=jnp.float32
    ).astype(jnp.int32)
    slot_numbers = jnp.sum(before * onehot, axis=1)
    return pair_ids * capacity + slot_numbers


def experts_layer(tokens_in, routing, logits, up_weight, down_weight, capacity):
    batch_count, row_count, feature_width = tokens_in.shape
    per_device = up_weight.shape[0]
    groups = lax.axis_size("expert")
    experts = per_device * groups
    slots_total = experts * capacity
    slot_block = per_device * capacity
    flats = jnp.stack([routing_slots(routing[0], experts, capacity)])
    row_ids = jnp.broadcast_to(
        jnp.arange(row_count, dtype=jnp.int32)[:, None], (row_count, TOP)
    ).reshape(-1)

    def fill_table(slot_index):
        return jnp.full((slots_total,), -1, jnp.int32).at[slot_index].set(row_ids)

    sources = jax.vmap(fill_table)(flats)
    offset = jnp.arange(batch_count, dtype=jnp.int32)[:, None] * row_count
    source_index = jnp.where(sources >= 0, sources + offset, -1)
    source_index = (
        source_index.reshape(batch_count, groups, slot_block).transpose(1, 0, 2).reshape(-1)
    )
    flat_tokens = tokens_in.reshape(batch_count * row_count, feature_width)
    outgoing = jnp.where(
        (source_index >= 0)[:, None],
        flat_tokens[jnp.maximum(source_index, 0)],
        jnp.zeros((), flat_tokens.dtype),
    )
    outgoing = outgoing.reshape(groups, batch_count, per_device, capacity, feature_width)
    arrived = lax.all_to_all(outgoing, "expert", split_axis=0, concat_axis=0, tiled=True)
    partial_value = jnp.einsum(
        "gmxcd,xdf->gmxcf", arrived, up_weight, preferred_element_type=jnp.float32
    )
    rounded = lax.optimization_barrier(partial_value.astype(jnp.bfloat16)).astype(jnp.float32)
    summed = lax.psum(rounded.astype(jnp.bfloat16), "dp").astype(jnp.float32)
    hidden = jax.nn.silu(summed).astype(jnp.bfloat16)
    produced = jnp.einsum(
        "gmxcf,xfd->gmxcd", hidden, down_weight, preferred_element_type=jnp.float32
    ).astype(jnp.bfloat16)
    returned = lax.all_to_all(produced, "expert", split_axis=0, concat_axis=0, tiled=True)
    pick_index = (
        flats // slot_block * (batch_count * slot_block)
        + jnp.arange(batch_count, dtype=jnp.int32)[:, None] * slot_block
        + flats % slot_block
    )
    gathered = returned.reshape(-1, feature_width)[pick_index.reshape(-1)].reshape(
        batch_count, row_count, TOP, feature_width
    )
    weights = gate_weights(logits)
    routed_sum = jnp.einsum("mrk,mrkd->mrd", weights, gathered.astype(jnp.float32))
    return (tokens_in.astype(jnp.float32) + routed_sum).astype(jnp.bfloat16)


def body(in_flight, incoming, up_proj, down_proj, expert_ids, gate_logits):
    up_weight = up_proj[0]
    down_weight = down_proj[0]
    groups = lax.axis_size("expert")
    row_count = in_flight.shape[2]
    per_device = up_weight.shape[0]
    capacity = max(2, 3 * row_count * TOP // (2 * per_device * groups))
    current = in_flight[0]
    is_first = lax.axis_index("section") == 0
    states = []
    for tick_index in range(TICKS):
        if tick_index > 0:
            handed_on = shifted(states[-1], "section", 1)
            current = jnp.where(is_first, incoming, handed_on)
        routing = expert_ids[tick_index, 0]
        logits = gate_logits[tick_index, 0]
        pieces = [
            experts_layer(
                current[micro_index : micro_index + 1],
                routing[micro_index : micro_index + 1],
                logits[micro_index : micro_index + 1],
                up_weight,
                down_weight,
                capacity,
            )
            for micro_index in range(MB)
        ]
        result = jnp.concatenate(pieces, axis=0)
        states.append(result)
    return jnp.stack(states)[:, None]


MESH = pl.DeviceIdType.MESH
LAG = 2
RING = 5


def relay_kernel(
    dims, x_ref, inc_ref, rt_ref, up_hbm, down_hbm, out_ref,
    x_all, x_disp, route, pick, blend, own, from_left, from_right, to_right, to_left,
    made, part_out, part_in, up, ring,
    up_sem, ring_sem, local_sem, tok_send, tok_recv, rt_send, rt_recv, hand_send, hand_recv,
    right_send, left_send, left_recv, right_recv, part_send, part_recv,
):
    sections, chain, rows, per_device, capacity = dims
    section = lax.axis_index("section")
    group = lax.axis_index("expert")
    spot = lax.axis_index("dp")
    other = 1 - group
    local = MB * rows
    slots = 2 * MB * capacity
    f32, bf16 = jnp.float32, jnp.bfloat16
    first_section = section == 0
    has_left, has_right = spot > 0, spot < chain - 1
    partner = (section, other, spot)
    my_rows = pl.ds(pl.multiple_of(group * local, local), local)

    def remote(src, dst, send, recv, device):
        return pltpu.make_async_remote_copy(
            src_ref=src, dst_ref=dst, send_sem=send, recv_sem=recv,
            device_id=device, device_id_type=MESH,
        )

    def load_up(e):
        return pltpu.make_async_copy(up_hbm.at[e], up.at[e], up_sem.at[e])

    def load_down(e, slot):
        return pltpu.make_async_copy(down_hbm.at[e], ring.at[slot], ring_sem.at[slot])

    for e in range(per_device):
        load_up(e).start()
    for e in range(min(RING, per_device)):
        load_down(e, e).start()
    keep_first = pltpu.make_async_copy(x_ref, x_all.at[0, my_rows], local_sem.at[0])
    keep_first.start()
    keep_second = pltpu.make_async_copy(inc_ref, x_all.at[1, my_rows], local_sem.at[1])

    @pl.when(first_section)
    def _():
        keep_second.start()

    keep_route = pltpu.make_async_copy(rt_ref, route.at[group], local_sem.at[2])
    keep_route.start()

    barrier = pltpu.get_barrier_semaphore()

    def greet(device):
        pl.semaphore_signal(barrier, inc=1, device_id=device, device_id_type=MESH)

    greet(partner)
    for condition, step in ((has_left, -1), (has_right, 1)):
        @pl.when(condition)
        def _(step=step):
            greet((section, group, spot + step))
    for condition, step in ((section > 0, -1), (section < sections - 1, 1)):
        @pl.when(condition)
        def _(step=step):
            greet((section + step, group, spot))
            greet((section + step, other, spot))
    peers = (
        1 + has_left.astype(jnp.int32) + has_right.astype(jnp.int32)
        + 2 * (section > 0).astype(jnp.int32) + 2 * (section < sections - 1).astype(jnp.int32)
    )
    pl.semaphore_wait(barrier, peers)

    send_route = remote(rt_ref, route.at[group], rt_send, rt_recv, partner)
    send_route.start()
    send_first = remote(x_ref, x_all.at[0, my_rows], tok_send.at[0], tok_recv.at[0], partner)
    send_first.start()
    send_second = remote(inc_ref, x_all.at[1, my_rows], tok_send.at[1], tok_recv.at[1], partner)

    @pl.when(first_section)
    def _():
        send_second.start()

    keep_route.wait()
    send_route.wait()

    def build_tables(tick):
        number = lax.broadcasted_iota(jnp.int32, (per_device, local), 0)
        wanted = (number + group * per_device).astype(f32)
        half = lax.broadcasted_iota(jnp.int32, (per_device, local), 1) // rows
        row_a = lax.broadcasted_iota(jnp.int32, (local, local), 0)
        row_b = lax.broadcasted_iota(jnp.int32, (local, local), 1)
        earlier = jnp.where(
            (row_a < row_b) & (row_a // rows == row_b // rows), 1.0, 0.0
        ).astype(bf16)
        slot_iota = lax.broadcasted_iota(jnp.int32, (slots, local), 0).astype(f32)
        for g in range(2):
            table = route[g, tick]
            squashed = 1.0 / (1.0 + jnp.exp(-table[TOP:]))
            gates = 2.5 * squashed / jnp.sum(squashed, axis=0, keepdims=True)
            named = jnp.zeros((per_device, local), f32)
            gate_of = jnp.zeros((per_device, local), f32)
            for k in range(TOP):
                hit = table[k : k + 1] == wanted
                named = named + jnp.where(hit, 1.0, 0.0)
                gate_of = gate_of + jnp.where(hit, gates[k : k + 1], 0.0)
            rank = jnp.dot(named.astype(bf16), earlier, preferred_element_type=f32)
            code = jnp.where(
                named > 0.5, rank + ((g * MB + half) * capacity).astype(f32), -1.0
            )
            for e in range(per_device):
                same = slot_iota == code[e : e + 1]
                pick[e * slots : (e + 1) * slots, g * local : (g + 1) * local] = jnp.where(
                    same, 1.0, 0.0
                ).astype(bf16)
                blend[g, e * slots : (e + 1) * slots, :] = jnp.where(
                    same, gate_of[e : e + 1], 0.0
                ).astype(bf16)

    def group_rows(j):
        return pl.ds(pl.multiple_of(j * slots, slots), slots)

    for tick in range(TICKS):
        build_tables(tick)
        if tick == 0:
            keep_first.wait()
            send_first.wait()
        else:
            @pl.when(first_section)
            def _():
                keep_second.wait()
                send_second.wait()

            @pl.when(section > 0)
            def _():
                for g in range(2):
                    remote(
                        x_ref, x_all.at[1, pl.ds(g * local, local)],
                        hand_send.at[g], hand_recv.at[g], partner,
                    ).wait_recv()
        x_disp[...] = jnp.dot(
            pick[...], x_all[tick], preferred_element_type=f32
        ).astype(bf16)

        def right_copy(j, tick=tick):
            return remote(
                to_right.at[group_rows(j)], from_left.at[tick, group_rows(j)],
                right_send.at[tick, j], left_recv.at[tick, j], (section, group, spot + 1),
            )

        def left_copy(j, tick=tick):
            return remote(
                to_left.at[group_rows(j)], from_right.at[tick, group_rows(j)],
                left_send.at[tick, j], right_recv.at[tick, j], (section, group, spot - 1),
            )

        def step(i, carry, tick=tick):
            @pl.when(i < per_device)
            def _():
                if tick == 0:
                    pltpu.make_async_copy(up_hbm.at[i], up.at[i], up_sem.at[i]).wait()
                own[group_rows(i), :] = jnp.dot(
                    x_disp[group_rows(i), :], up[i], preferred_element_type=f32
                ).astype(bf16)

            to_r = i - LAG * spot

            @pl.when(has_right & (to_r >= 0) & (to_r < per_device))
            def _():
                @pl.when(has_left)
                def _():
                    right_copy(to_r).wait_recv()
                    to_right[group_rows(to_r), :] = (
                        own[group_rows(to_r), :].astype(f32)
                        + from_left[tick, group_rows(to_r), :].astype(f32)
                    ).astype(bf16)

                @pl.when(spot == 0)
                def _():
                    to_right[group_rows(to_r), :] = own[group_rows(to_r), :]

                right_copy(to_r).start()

            to_l = i - LAG * (chain - 1 - spot)

            @pl.when(has_left & (to_l >= 0) & (to_l < per_device))
            def _():
                @pl.when(has_right)
                def _():
                    left_copy(to_l).wait_recv()
                    to_left[group_rows(to_l), :] = (
                        own[group_rows(to_l), :].astype(f32)
                        + from_right[tick, group_rows(to_l), :].astype(f32)
                    ).astype(bf16)

                @pl.when(spot == chain - 1)
                def _():
                    to_left[group_rows(to_l), :] = own[group_rows(to_l), :]

                left_copy(to_l).start()

            last = i - LAG * (chain - 1)

            @pl.when(last >= 0)
            def _():
                turn = tick * per_device + last
                slot = turn % RING
                block = group_rows(last)

                @pl.when(spot == chain - 1)
                def _():
                    right_copy(last).wait_recv()
                    own[block, :] = (
                        own[block, :].astype(f32) + from_left[tick, block, :].astype(f32)
                    ).astype(bf16)

                @pl.when(spot == 0)
                def _():
                    left_copy(last).wait_recv()
                    own[block, :] = (
                        own[block, :].astype(f32) + from_right[tick, block, :].astype(f32)
                    ).astype(bf16)

                @pl.when(has_left & has_right)
                def _():
                    own[block, :] = (
                        to_right[block, :].astype(f32) + from_right[tick, block, :].astype(f32)
                    ).astype(bf16)

                total = own[block, :].astype(f32)
                hidden = (total / (1.0 + jnp.exp(-total))).astype(bf16)
                load_down(last, slot).wait()
                made[block, :] = jnp.dot(
                    hidden, ring[slot], preferred_element_type=f32
                ).astype(bf16)

                @pl.when(turn + RING < TICKS * per_device)
                def _():
                    load_down((last + RING) % per_device, slot).start()

            return carry

        lax.fori_loop(0, per_device + LAG * (chain - 1), step, 0)

        def combined(g):
            return lax.dot_general(
                blend[g], made[...], (((0,), (0,)), ((), ())), preferred_element_type=f32
            )

        part_out[tick] = combined(other).astype(bf16)
        send_part = remote(
            part_out.at[tick], part_in.at[tick], part_send.at[tick], part_recv.at[tick], partner
        )
        send_part.start()
        mine = x_all[tick, my_rows, :].astype(f32) + combined(group)
        send_part.wait()
        out_ref[tick] = (mine + part_in[tick].astype(f32)).astype(bf16)

        if tick + 1 < TICKS:
            @pl.when(section < sections - 1)
            def _():
                for g, send in ((group, 0), (other, 1)):
                    remote(
                        out_ref.at[tick], x_all.at[1, my_rows], hand_send.at[send],
                        hand_recv.at[group], (section + 1, g, spot),
                    ).start()

        def settle(j, carry):
            @pl.when(has_right)
            def _():
                right_copy(j).wait_send()

            @pl.when(has_left)
            def _():
                left_copy(j).wait_send()

            return carry

        lax.fori_loop(0, per_device, settle, 0)

    @pl.when(section < sections - 1)
    def _():
        for g, send in ((group, 0), (other, 1)):
            remote(
                out_ref.at[0], x_all.at[1, my_rows], hand_send.at[send],
                hand_recv.at[group], (section + 1, g, spot),
            ).wait_send()


def relay_body(sections, chain, in_flight, incoming, up_proj, down_proj, expert_ids, gate_logits):
    _, _, rows, width = in_flight.shape
    _, per_device, _, ff = up_proj.shape
    capacity = max(2, 3 * rows * TOP // (2 * per_device * 2))
    local = MB * rows
    slots = 2 * MB * capacity
    every = per_device * slots
    bf16, f32 = jnp.bfloat16, jnp.float32
    routing = jnp.concatenate(
        [
            expert_ids[:, 0].astype(f32).reshape(TICKS, local, TOP).transpose(0, 2, 1),
            gate_logits[:, 0].reshape(TICKS, local, TOP).transpose(0, 2, 1),
        ],
        axis=1,
    )
    vmem = pl.BlockSpec(memory_space=pltpu.VMEM)
    anywhere = pl.BlockSpec(memory_space=pl.ANY)
    dma = pltpu.SemaphoreType.DMA
    states = pl.pallas_call(
        functools.partial(relay_kernel, (sections, chain, rows, per_device, capacity)),
        out_shape=jax.ShapeDtypeStruct((TICKS, local, width), bf16),
        in_specs=[vmem, vmem, vmem, anywhere, anywhere],
        out_specs=vmem,
        scratch_shapes=[
            pltpu.VMEM((TICKS, 2 * local, width), bf16),
            pltpu.VMEM((every, width), bf16),
            pltpu.VMEM((2, TICKS, 2 * TOP, local), f32),
            pltpu.VMEM((every, 2 * local), bf16),
            pltpu.VMEM((2, every, local), bf16),
            pltpu.VMEM((every, ff), bf16),
            pltpu.VMEM((TICKS, every, ff), bf16),
            pltpu.VMEM((TICKS, every, ff), bf16),
            pltpu.VMEM((every, ff), bf16),
            pltpu.VMEM((every, ff), bf16),
            pltpu.VMEM((every, width), bf16),
            pltpu.VMEM((TICKS, local, width), bf16),
            pltpu.VMEM((TICKS, local, width), bf16),
            pltpu.VMEM((per_device, width, ff), bf16),
            pltpu.VMEM((RING, ff, width), bf16),
            dma((per_device,)),
            dma((RING,)),
            dma((3,)),
            dma((2,)),
            dma((2,)),
            dma,
            dma,
            dma((2,)),
            dma((2,)),
            dma((TICKS, per_device)),
            dma((TICKS, per_device)),
            dma((TICKS, per_device)),
            dma((TICKS, per_device)),
            dma((TICKS,)),
            dma((TICKS,)),
        ],
        compiler_params=pltpu.CompilerParams(
            collective_id=0, has_side_effects=True, vmem_limit_bytes=63 * 1024 * 1024
        ),
    )(
        in_flight.reshape(local, width),
        incoming.reshape(local, width),
        routing,
        up_proj[0],
        down_proj[0],
    )
    return states.reshape(TICKS, 1, MB, rows, width)


def solution(mesh):
    shape = dict(mesh.shape)
    if shape["expert"] == 2:
        layer = functools.partial(relay_body, shape["section"], shape["dp"])
    else:
        layer = body
    return jax.shard_map(
        layer,
        mesh=mesh,
        in_specs=(
            P("section", None, "expert", "dp"),
            P(None, "expert", "dp"),
            P("section", "expert", "dp", None),
            P("section", "expert", None, "dp"),
            P(None, "section", None, "expert", None),
            P(None, "section", None, "expert", None),
        ),
        out_specs=P(None, "section", None, "expert", "dp"),
        check_vma=False,
    )
```

```python
import functools

import jax
import jax.numpy as jnp
from jax import lax
from jax.experimental import pallas as pl
from jax.experimental.pallas import tpu as pltpu
from jax.sharding import PartitionSpec as P

MB = 2
TICKS = 2
TOP = 4


def shifted(block, axis, distance):
    devices = range(lax.axis_size(axis))
    route = [(i - distance, i) for i in devices if i - distance in devices]
    return lax.ppermute(block, axis, route)


def gate_weights(logits):
    squashed = jax.nn.sigmoid(logits)
    return 2.5 * squashed / jnp.sum(squashed, axis=-1, keepdims=True)


def routing_slots(routing, experts, capacity):
    pair_ids = routing.reshape(-1)
    onehot = (pair_ids[:, None] == jnp.arange(experts, dtype=jnp.int32)[None, :]).astype(jnp.int32)
    earlier = jnp.tri(pair_ids.shape[0], k=-1, dtype=jnp.bfloat16)
    before = jnp.dot(
        earlier, onehot.astype(jnp.bfloat16), preferred_element_type=jnp.float32
    ).astype(jnp.int32)
    slot_numbers = jnp.sum(before * onehot, axis=1)
    return pair_ids * capacity + slot_numbers


def experts_layer(tokens_in, routing, logits, up_weight, down_weight, capacity):
    batch_count, row_count, feature_width = tokens_in.shape
    per_device = up_weight.shape[0]
    groups = lax.axis_size("expert")
    experts = per_device * groups
    slots_total = experts * capacity
    slot_block = per_device * capacity
    flats = jnp.stack([routing_slots(routing[0], experts, capacity)])
    row_ids = jnp.broadcast_to(
        jnp.arange(row_count, dtype=jnp.int32)[:, None], (row_count, TOP)
    ).reshape(-1)

    def fill_table(slot_index):
        return jnp.full((slots_total,), -1, jnp.int32).at[slot_index].set(row_ids)

    sources = jax.vmap(fill_table)(flats)
    offset = jnp.arange(batch_count, dtype=jnp.int32)[:, None] * row_count
    source_index = jnp.where(sources >= 0, sources + offset, -1)
    source_index = (
        source_index.reshape(batch_count, groups, slot_block).transpose(1, 0, 2).reshape(-1)
    )
    flat_tokens = tokens_in.reshape(batch_count * row_count, feature_width)
    outgoing = jnp.where(
        (source_index >= 0)[:, None],
        flat_tokens[jnp.maximum(source_index, 0)],
        jnp.zeros((), flat_tokens.dtype),
    )
    outgoing = outgoing.reshape(groups, batch_count, per_device, capacity, feature_width)
    arrived = lax.all_to_all(outgoing, "expert", split_axis=0, concat_axis=0, tiled=True)
    partial_value = jnp.einsum(
        "gmxcd,xdf->gmxcf", arrived, up_weight, preferred_element_type=jnp.float32
    )
    rounded = lax.optimization_barrier(partial_value.astype(jnp.bfloat16)).astype(jnp.float32)
    summed = lax.psum(rounded.astype(jnp.bfloat16), "dp").astype(jnp.float32)
    hidden = jax.nn.silu(summed).astype(jnp.bfloat16)
    produced = jnp.einsum(
        "gmxcf,xfd->gmxcd", hidden, down_weight, preferred_element_type=jnp.float32
    ).astype(jnp.bfloat16)
    returned = lax.all_to_all(produced, "expert", split_axis=0, concat_axis=0, tiled=True)
    pick_index = (
        flats // slot_block * (batch_count * slot_block)
        + jnp.arange(batch_count, dtype=jnp.int32)[:, None] * slot_block
        + flats % slot_block
    )
    gathered = returned.reshape(-1, feature_width)[pick_index.reshape(-1)].reshape(
        batch_count, row_count, TOP, feature_width
    )
    weights = gate_weights(logits)
    routed_sum = jnp.einsum("mrk,mrkd->mrd", weights, gathered.astype(jnp.float32))
    return (tokens_in.astype(jnp.float32) + routed_sum).astype(jnp.bfloat16)


def body(in_flight, incoming, up_proj, down_proj, expert_ids, gate_logits):
    up_weight = up_proj[0]
    down_weight = down_proj[0]
    groups = lax.axis_size("expert")
    row_count = in_flight.shape[2]
    per_device = up_weight.shape[0]
    capacity = max(2, 3 * row_count * TOP // (2 * per_device * groups))
    current = in_flight[0]
    is_first = lax.axis_index("section") == 0
    states = []
    for tick_index in range(TICKS):
        if tick_index > 0:
            handed_on = shifted(states[-1], "section", 1)
            current = jnp.where(is_first, incoming, handed_on)
        routing = expert_ids[tick_index, 0]
        logits = gate_logits[tick_index, 0]
        pieces = [
            experts_layer(
                current[micro_index : micro_index + 1],
                routing[micro_index : micro_index + 1],
                logits[micro_index : micro_index + 1],
                up_weight,
                down_weight,
                capacity,
            )
            for micro_index in range(MB)
        ]
        result = jnp.concatenate(pieces, axis=0)
        states.append(result)
    return jnp.stack(states)[:, None]


MESH = pl.DeviceIdType.MESH
LAG = 2
RING = 5
UNITS = TICKS * MB


def relay_kernel(
    dims, x_ref, inc_ref, rt_ref, up_hbm, down_hbm, out_ref,
    x_all, x_disp, route, pick, blend, own, from_left, from_right, to_right, to_left,
    made, gathered, part_out, part_in, up, ring,
    up_sem, ring_sem, local_sem, tok_send, tok_recv, rt_send, rt_recv, hand_send, hand_recv,
    right_send, left_send, left_recv, right_recv, part_send, part_recv,
):
    sections, chain, rows, per_device, capacity = dims
    section = lax.axis_index("section")
    group = lax.axis_index("expert")
    spot = lax.axis_index("dp")
    other = 1 - group
    slots = 2 * capacity
    pair_rows = 2 * slots
    padded = (slots + 15) // 16 * 16
    pairs = per_device // 2
    total_groups = UNITS * pairs
    kept = 2 * pairs
    f32, bf16 = jnp.float32, jnp.bfloat16
    has_left, has_right = spot > 0, spot < chain - 1
    partner = (section, other, spot)
    my_rows = pl.ds(pl.multiple_of(group * rows, rows), rows)
    other_rows = pl.ds(pl.multiple_of(other * rows, rows), rows)

    def remote(src, dst, send, recv, device):
        return pltpu.make_async_remote_copy(
            src_ref=src, dst_ref=dst, send_sem=send, recv_sem=recv,
            device_id=device, device_id_type=MESH,
        )

    def load_up(e):
        return pltpu.make_async_copy(up_hbm.at[e], up.at[e], up_sem.at[e])

    def load_down(e, slot):
        return pltpu.make_async_copy(down_hbm.at[e], ring.at[slot], ring_sem.at[slot])

    for e in range(per_device):
        load_up(e).start()
    for e in range(min(RING, per_device)):
        load_down(e, e).start()
    def source(u):
        return x_ref.at[u] if u < MB else inc_ref.at[u - MB]

    def keep(u):
        return pltpu.make_async_copy(source(u), x_all.at[u, my_rows], local_sem.at[u])

    def exchange(u):
        return remote(
            source(u), x_all.at[u, my_rows], tok_send.at[u], tok_recv.at[u], partner
        )

    first_section = section == 0
    for u in range(UNITS):
        if u < MB:
            keep(u).start()
        else:
            @pl.when(first_section)
            def _(u=u):
                keep(u).start()

    keep_route = pltpu.make_async_copy(rt_ref, route.at[group], local_sem.at[UNITS])
    keep_route.start()

    barrier = pltpu.get_barrier_semaphore()

    def greet(device):
        pl.semaphore_signal(barrier, inc=1, device_id=device, device_id_type=MESH)

    greet(partner)
    for condition, step in ((has_left, -1), (has_right, 1)):
        @pl.when(condition)
        def _(step=step):
            greet((section, group, spot + step))
    for condition, step in ((section > 0, -1), (section < sections - 1, 1)):
        @pl.when(condition)
        def _(step=step):
            greet((section + step, group, spot))
            greet((section + step, other, spot))
    peers = (
        1 + has_left.astype(jnp.int32) + has_right.astype(jnp.int32)
        + 2 * (section > 0).astype(jnp.int32) + 2 * (section < sections - 1).astype(jnp.int32)
    )
    pl.semaphore_wait(barrier, peers)

    send_route = remote(rt_ref, route.at[group], rt_send, rt_recv, partner)
    send_route.start()
    for u in range(UNITS):
        if u < MB:
            exchange(u).start()
        else:
            @pl.when(first_section)
            def _(u=u):
                exchange(u).start()

    keep_route.wait()
    send_route.wait()

    def build_tables(u):
        local = 2 * rows
        number = lax.broadcasted_iota(jnp.int32, (per_device, local), 0)
        wanted = (number + group * per_device).astype(f32)
        lane = lax.broadcasted_iota(jnp.int32, (per_device, local), 1)
        row_a = lax.broadcasted_iota(jnp.int32, (local, local), 0)
        row_b = lax.broadcasted_iota(jnp.int32, (local, local), 1)
        earlier = jnp.where(
            (row_a < row_b) & (row_a // rows == row_b // rows), 1.0, 0.0
        ).astype(bf16)
        table_lane = lax.broadcasted_iota(jnp.int32, (2 * TOP, local), 1)
        table = jnp.where(table_lane < rows, route[0, u], route[1, u])
        squashed = 1.0 / (1.0 + jnp.exp(-table[TOP:]))
        gates = 2.5 * squashed / jnp.sum(squashed, axis=0, keepdims=True)
        named = jnp.zeros((per_device, local), f32)
        gate_of = jnp.zeros((per_device, local), f32)
        for k in range(TOP):
            hit = table[k : k + 1] == wanted
            named = named + jnp.where(hit, 1.0, 0.0)
            gate_of = gate_of + jnp.where(hit, gates[k : k + 1], 0.0)
        rank = jnp.dot(named.astype(bf16), earlier, preferred_element_type=f32)
        code = jnp.where(
            named > 0.5, rank + jnp.where(lane < rows, 0.0, float(capacity)), -1000.0
        )
        wide = lax.broadcasted_iota(jnp.int32, (2 * padded, local), 0).astype(f32)
        tight = lax.broadcasted_iota(jnp.int32, (pair_rows, local), 0).astype(f32)
        for p in range(pairs):
            one, two = code[2 * p : 2 * p + 1], code[2 * p + 1 : 2 * p + 2]
            pick[2 * p * padded : 2 * (p + 1) * padded, :] = (
                jnp.where(wide == one, 1.0, 0.0) + jnp.where(wide - float(padded) == two, 1.0, 0.0)
            ).astype(bf16)
            blend[u, p * pair_rows : (p + 1) * pair_rows, :] = (
                jnp.where(tight == one, gate_of[2 * p : 2 * p + 1], 0.0)
                + jnp.where(tight - float(slots) == two, gate_of[2 * p + 1 : 2 * p + 2], 0.0)
            ).astype(bf16)

    def kept_rows(j):
        return pl.ds(pl.multiple_of((j % kept) * pair_rows, pair_rows), pair_rows)

    def right_copy(j):
        return remote(
            to_right.at[kept_rows(j)], from_left.at[j],
            right_send.at[j], left_recv.at[j], (section, group, spot + 1),
        )

    def left_copy(j):
        return remote(
            to_left.at[kept_rows(j)], from_right.at[j],
            left_send.at[j], right_recv.at[j], (section, group, spot - 1),
        )

    def part_copy(u):
        return remote(part_out.at[u], part_in.at[u], part_send.at[u], part_recv.at[u], partner)

    def hand_copy(m, g, which):
        return remote(
            out_ref.at[m], x_all.at[m + MB, my_rows], hand_send.at[m, which],
            hand_recv.at[m, group], (section + 1, g, spot),
        )

    deep = LAG * (chain - 1)

    def step(i, carry):
        for u in range(UNITS):
            @pl.when(i == u * pairs)
            def _(u=u):
                if u < MB:
                    keep(u).wait()
                    exchange(u).wait()
                else:
                    @pl.when(first_section)
                    def _():
                        keep(u).wait()
                        exchange(u).wait()

                    @pl.when(section > 0)
                    def _():
                        for g in range(2):
                            remote(
                                x_ref.at[0], x_all.at[u, pl.ds(g * rows, rows)],
                                hand_send.at[u - MB, g], hand_recv.at[u - MB, g], partner,
                            ).wait_recv()

        @pl.when((i < total_groups) & (i % pairs == 0))
        def _():
            u = i // pairs
            build_tables(u)
            x_disp[...] = jnp.dot(
                pick[...], x_all[u], preferred_element_type=f32
            ).astype(bf16)

        @pl.when(i < total_groups)
        def _():
            pair = i % pairs

            @pl.when(i < pairs)
            def _():
                for t in range(2):
                    e = 2 * pair + t
                    pltpu.make_async_copy(up_hbm.at[e], up.at[e], up_sem.at[e]).wait()

            halves = []
            for t in range(2):
                e = 2 * pair + t
                block = x_disp[pl.ds(pl.multiple_of(e * padded, padded), padded), :]
                halves.append(jnp.dot(block, up[e], preferred_element_type=f32)[:slots])
            own[kept_rows(i), :] = jnp.concatenate(halves, axis=0).astype(bf16)

        to_r = i - LAG * spot

        @pl.when(has_right & (to_r >= 0) & (to_r < total_groups))
        def _():
            @pl.when(to_r >= kept)
            def _():
                right_copy(to_r - kept).wait_send()

            @pl.when(has_left)
            def _():
                right_copy(to_r).wait_recv()
                to_right[kept_rows(to_r), :] = (
                    own[kept_rows(to_r), :].astype(f32) + from_left[to_r].astype(f32)
                ).astype(bf16)

            @pl.when(spot == 0)
            def _():
                to_right[kept_rows(to_r), :] = own[kept_rows(to_r), :]

            right_copy(to_r).start()

        to_l = i - LAG * (chain - 1 - spot)

        @pl.when(has_left & (to_l >= 0) & (to_l < total_groups))
        def _():
            @pl.when(to_l >= kept)
            def _():
                left_copy(to_l - kept).wait_send()

            @pl.when(has_right)
            def _():
                left_copy(to_l).wait_recv()
                to_left[kept_rows(to_l), :] = (
                    own[kept_rows(to_l), :].astype(f32) + from_right[to_l].astype(f32)
                ).astype(bf16)

            @pl.when(spot == chain - 1)
            def _():
                to_left[kept_rows(to_l), :] = own[kept_rows(to_l), :]

            left_copy(to_l).start()

        last = i - deep

        @pl.when((last >= 0) & (last < total_groups))
        def _():
            block = kept_rows(last)

            @pl.when(spot == chain - 1)
            def _():
                right_copy(last).wait_recv()
                own[block, :] = (
                    own[block, :].astype(f32) + from_left[last].astype(f32)
                ).astype(bf16)

            @pl.when(spot == 0)
            def _():
                left_copy(last).wait_recv()
                own[block, :] = (
                    own[block, :].astype(f32) + from_right[last].astype(f32)
                ).astype(bf16)

            @pl.when(has_left & has_right)
            def _():
                own[block, :] = (
                    to_right[block, :].astype(f32) + from_right[last].astype(f32)
                ).astype(bf16)

            total = own[block, :].astype(f32)
            hidden = total / (1.0 + jnp.exp(-total))
            halves = []
            for t in range(2):
                turn = 2 * last + t
                slot = turn % RING
                load_down(turn % per_device, slot).wait()
                halves.append(jnp.dot(
                    hidden[t * slots : (t + 1) * slots].astype(bf16), ring[slot],
                    preferred_element_type=f32,
                ))
            made[kept_rows(last), :] = jnp.concatenate(halves, axis=0).astype(bf16)
            for t in range(2):
                turn = 2 * last + t

                @pl.when(turn + RING < 2 * total_groups)
                def _(turn=turn):
                    load_down((turn + RING) % per_device, turn % RING).start()

        @pl.when((last >= pairs) & (last % pairs == 0) & (last <= total_groups))
        def _():
            u = last // pairs - 1
            part_copy(u).wait()
            result = (
                x_all[u, my_rows, :].astype(f32)
                + gathered[my_rows, :]
                + part_in[u].astype(f32)
            )
            out_ref[u] = result.astype(bf16)

            @pl.when((u < UNITS - MB) & (section < sections - 1))
            def _():
                hand_copy(u, group, 0).start()
                hand_copy(u, other, 1).start()

        @pl.when((last >= 0) & (last < total_groups) & (last % pairs == pairs - 1))
        def _():
            u = last // pairs
            span = pairs * pair_rows
            output = made[pl.ds(pl.multiple_of((u % 2) * span, span), span), :]
            gathered[...] = lax.dot_general(
                blend[u], output, (((0,), (0,)), ((), ())), preferred_element_type=f32
            )
            part_out[u] = gathered[other_rows, :].astype(bf16)
            part_copy(u).start()

        return carry

    lax.fori_loop(0, total_groups + deep + 1, step, 0)

    def settle(j, carry):
        @pl.when(has_right)
        def _():
            right_copy(j).wait_send()

        @pl.when(has_left)
        def _():
            left_copy(j).wait_send()

        return carry

    lax.fori_loop(total_groups - kept, total_groups, settle, 0)

    @pl.when(section < sections - 1)
    def _():
        for m in range(UNITS - MB):
            hand_copy(m, group, 0).wait_send()
            hand_copy(m, other, 1).wait_send()


def relay_body(sections, chain, in_flight, incoming, up_proj, down_proj, expert_ids, gate_logits):
    _, _, rows, width = in_flight.shape
    _, per_device, _, ff = up_proj.shape
    capacity = max(2, 3 * rows * TOP // (2 * per_device * 2))
    slots = 2 * capacity
    padded = (slots + 15) // 16 * 16
    pairs = per_device // 2
    every = per_device * slots
    bf16, f32 = jnp.bfloat16, jnp.float32
    routing = jnp.concatenate(
        [
            expert_ids[:, 0].astype(f32).reshape(UNITS, rows, TOP).transpose(0, 2, 1),
            gate_logits[:, 0].reshape(UNITS, rows, TOP).transpose(0, 2, 1),
        ],
        axis=1,
    )
    routing = jnp.concatenate([routing, routing], axis=2)
    vmem = pl.BlockSpec(memory_space=pltpu.VMEM)
    anywhere = pl.BlockSpec(memory_space=pl.ANY)
    dma = pltpu.SemaphoreType.DMA
    states = pl.pallas_call(
        functools.partial(relay_kernel, (sections, chain, rows, per_device, capacity)),
        out_shape=jax.ShapeDtypeStruct((UNITS, rows, width), bf16),
        in_specs=[vmem, vmem, vmem, anywhere, anywhere],
        out_specs=vmem,
        scratch_shapes=[
            pltpu.VMEM((UNITS, 2 * rows, width), bf16),
            pltpu.VMEM((per_device * padded, width), bf16),
            pltpu.VMEM((2, UNITS, 2 * TOP, 2 * rows), f32),
            pltpu.VMEM((per_device * padded, 2 * rows), bf16),
            pltpu.VMEM((UNITS, every, 2 * rows), bf16),
            pltpu.VMEM((2 * every, ff), bf16),
            pltpu.VMEM((UNITS * pairs, 2 * slots, ff), bf16),
            pltpu.VMEM((UNITS * pairs, 2 * slots, ff), bf16),
            pltpu.VMEM((2 * every, ff), bf16),
            pltpu.VMEM((2 * every, ff), bf16),
            pltpu.VMEM((2 * every, width), bf16),
            pltpu.VMEM((2 * rows, width), f32),
            pltpu.VMEM((UNITS, rows, width), bf16),
            pltpu.VMEM((UNITS, rows, width), bf16),
            pltpu.VMEM((per_device, width, ff), bf16),
            pltpu.VMEM((RING, ff, width), bf16),
            dma((per_device,)),
            dma((RING,)),
            dma((UNITS + 1,)),
            dma((UNITS,)),
            dma((UNITS,)),
            dma,
            dma,
            dma((UNITS - MB, 2)),
            dma((UNITS - MB, 2)),
            dma((UNITS * pairs,)),
            dma((UNITS * pairs,)),
            dma((UNITS * pairs,)),
            dma((UNITS * pairs,)),
            dma((UNITS,)),
            dma((UNITS,)),
        ],
        compiler_params=pltpu.CompilerParams(
            collective_id=0, has_side_effects=True, vmem_limit_bytes=63 * 1024 * 1024
        ),
    )(
        in_flight[0],
        incoming,
        routing,
        up_proj[0],
        down_proj[0],
    )
    return states.reshape(TICKS, 1, MB, rows, width)


def solution(mesh):
    shape = dict(mesh.shape)
    if shape["expert"] == 2:
        layer = functools.partial(relay_body, shape["section"], shape["dp"])
    else:
        layer = body
    return jax.shard_map(
        layer,
        mesh=mesh,
        in_specs=(
            P("section", None, "expert", "dp"),
            P(None, "expert", "dp"),
            P("section", "expert", "dp", None),
            P("section", "expert", None, "dp"),
            P(None, "section", None, "expert", None),
            P(None, "section", None, "expert", None),
        ),
        out_specs=P(None, "section", None, "expert", "dp"),
        check_vma=False,
    )
```
